32 devices in a mesh: groups: 2 (over y), block: 4 (over x, core), slab: 4 (over z).
Axes of the slice: x: 2, y: 2, z: 4, core: 2. Of those that a mesh axis runs over, the one named last changes fastest.
Arguments:
- point_coords: float32 [3, 131072], P(None, ('groups', 'block', 'slab')), parts along dimension 1, may hold values from -1 to 1
- point_normals: float32 [3, 131072], P(None, ('groups', 'block', 'slab')), parts along dimension 1, may hold values from -4 to 4
- strengths: float32 [2, 131072], P(None, ('groups', 'block', 'slab')), parts along dimension 1, may hold values from -1.2 to 1.2
- point_counts: int32 [32, 256], P(('groups', 'block', 'slab')), parts along dimension 0, may hold values from 1 to 16, 2560 in all within a row
- leaf_list: int32 [8192, 316], P(('groups', 'block', 'slab')), parts along dimension 0, may hold values from 0 to 1, as said below
- parent_list: int32 [1024, 316], P(('groups', 'block', 'slab')), parts along dimension 0, may hold values from 0 to 1, as said below
- summit_list: int32 [128, 316], P(('groups', 'block', 'slab')), parts along dimension 0, may hold values from 0 to 1, as said below
- translations: float32 [316, 32, 32], replicated, may hold values from -0.078125 to 0.078125
- compress: float32 [216, 32], replicated, may hold values from -0.4375 to 0.4375
- expand: float32 [216, 32], replicated, may hold values from -1 to 1
Outputs:
- potential: float32 [2, 131072], P(None, ('groups', 'block', 'slab')), parts along dimension 1
The draws below stay inside these ranges and needn't reach their ends.
There are 2 independent parts, one for each index of `groups`. The reference program is written for one: setup_inputs(seed, part) draws one part's arguments, and reference() takes and returns one part's arrays. A program takes and returns all parts, laid end to end along the dimension named above; an argument that names none is the same for every part. Nothing has to cross between parts.
Inputs may be any that keep to these rules, and one draw needn't show every extreme that they name: `leaf_list`: 1 where the box at that offset is in the target box's far-field list of the level; a box is listed only where its parent neighbours the target's parent. `parent_list`: as leaf_list, one level up. `summit_list`: as leaf_list, two levels up.
All inputs are finite; a program needn't handle non-finite values.
Results may differ from the reference program's by a relative error of at most 0.0003.
Values sent between devices are 32-bit elements; how exact they have to be, the bound alone decides.
A program may use at most 128 MiB of HBM per device.

```python
import math
import jax
import jax.numpy as jnp
import numpy as np
from jax import lax

ORDER = 6
RANK = 32
RHS = 2
OFFSETS = 316
BX = 8
BZ = 8
SY = 4
PCAP = 16
NODES = 216
DEVS = 16
LEAF_DEV = 256
LEAVES = 4096
PARENTS = 512
TOPS = 64
POINTS = 65536
PTS_LIVE = 2560
N_BLOCK = 4
N_SLAB = 4


def offset_list_drawn():
    listing = []
    for shift_x in range(-3, 4):
        for shift_y in range(-3, 4):
            for shift_z in range(-3, 4):
                if max(abs(shift_x), abs(shift_y), abs(shift_z)) > 1:
                    listing.append((shift_x, shift_y, shift_z))
    return listing


def list_mask(key, boxes, extent_x, extent_z, extent_y):
    row_ids = jnp.arange(boxes, dtype=jnp.int32)
    within = row_ids % (extent_x * extent_z * extent_y)
    place_x = within // (extent_z * extent_y)
    place_z = within // extent_y % extent_z
    place_y = within % extent_y
    shifts = jnp.array(offset_list_drawn(), dtype=jnp.int32)
    near_x = jnp.abs(jnp.floor_divide(place_x[:, None] % 2 + shifts[None, :, 0], 2)) <= 1
    near_y = jnp.abs(jnp.floor_divide(place_y[:, None] % 2 + shifts[None, :, 1], 2)) <= 1
    near_z = jnp.abs(jnp.floor_divide(place_z[:, None] % 2 + shifts[None, :, 2], 2)) <= 1
    kept_mask = jax.random.randint(key, (boxes, shifts.shape[0]), 0, 8) > 0
    return (near_x & near_y & near_z & kept_mask).astype(jnp.int32)


def draw_leaf_list(key, part):
    key = jax.random.fold_in(key, 11)
    return list_mask(key, LEAVES, BX, BZ, SY)


def draw_parent_list(key, part):
    key = jax.random.fold_in(key, 12)
    return list_mask(key, PARENTS, BX // 2, BZ // 2, SY // 2)


def draw_summit_list(key, part):
    key = jax.random.fold_in(key, 13)
    return list_mask(key, TOPS, BX // 4, BZ // 4, SY // 4)


def block_scale(stream_key, extent, split, low, high):
    def one(dim, blocks):
        steps = jax.random.uniform(jax.random.fold_in(jax.random.fold_in(stream_key, 6), dim), (blocks,), jnp.float32, low / len(split), high / len(split))
        return jnp.repeat(jnp.exp(steps), extent[dim] // blocks).reshape((-1,) + (1,) * (len(extent) - dim - 1))

    factor_of = one(*split[0])
    for cut in split[1:]:
        factor_of = factor_of * one(*cut)
    return factor_of


def split_up(count, total, bound, lean):
    weights = [(1 << 20) // math.isqrt(rank ** lean) + 1 for rank in range(2, count + 1)]
    rest, counts = total - bound - (count - 1), [1] * (count - 1)
    while rest > 0:
        free = [i for i in range(count - 1) if counts[i] < bound]
        whole, left = sum([weights[i] for i in free]), rest
        for i in free:
            extra = min(bound - counts[i], max(1, left * weights[i] // whole), rest)
            counts[i] = counts[i] + extra
            rest = rest - extra
    return np.array([bound] + counts)


def uneven(own_key, amount, total, bound, lean):
    if amount == 2:
        one = jax.random.randint(own_key, (), max(1, total - bound), min(bound, total - 1) + 1)
        return jnp.stack([one, total - one])
    sizes = jnp.asarray(split_up(amount, total, bound, lean), jnp.int32)
    pairs = (amount - 1) // 2
    donor, sink = sizes[1:1 + 2 * pairs:2], sizes[2:2 + 2 * pairs:2]
    slack = jnp.minimum(donor - 1, bound - sink)
    shifted = jax.random.randint(jax.random.fold_in(own_key, 1), (pairs,), 0, 1 << 20) % (slack + 1)
    sizes = sizes.at[1:1 + 2 * pairs:2].set(donor - shifted).at[2:2 + 2 * pairs:2].set(sink + shifted)
    return sizes[jax.random.permutation(jax.random.fold_in(own_key, 2), amount)]


def gaussian(stream_key, dims, scale, bound, shards=(), held_as=jnp.bfloat16):
    values = jax.random.normal(stream_key, dims, jnp.float32) * scale
    if len(shards) > 0:
        values = block_scale(stream_key, dims, shards, -0.22, 0.18) * values
    return jnp.clip(values, min=-bound, max=bound).astype(held_as)


def setup_inputs(seed: int = 0, part: int = 0) -> dict:
    key_list = jax.random.split(jax.random.key(seed), 11)
    part_splits = jax.random.split(jax.random.fold_in(key_list[10], part), 11)
    return {
        "point_coords": jnp.clip(jax.random.uniform(part_splits[0], (3, POINTS), jnp.float32, -1.0, 1.0) * block_scale(part_splits[0], (3, POINTS), ((1, 16),), -0.4, 0.0), -1.0, 1.0),
        "point_normals": gaussian(part_splits[1], (3, POINTS), 1.0, 4.0, ((1, 16),), jnp.float32),
        "strengths": gaussian(part_splits[2], (RHS, POINTS), 0.2, 1.2, ((1, 16),), jnp.float32),
        "point_counts": jax.vmap(lambda own: uneven(own, LEAF_DEV, PTS_LIVE, PCAP, 2))(jax.random.split(part_splits[3], DEVS)).reshape((DEVS, LEAF_DEV)).astype(jnp.int32),
        "leaf_list": draw_leaf_list(jax.random.fold_in(jax.random.fold_in(key_list[10], part), 71), part),
        "parent_list": draw_parent_list(jax.random.fold_in(jax.random.fold_in(key_list[10], part), 71), part),
        "summit_list": draw_summit_list(jax.random.fold_in(jax.random.fold_in(key_list[10], part), 71), part),
        "translations": gaussian(key_list[7], (OFFSETS, RANK, RANK), (RANK * 160) ** -0.5, 0.078125, (), jnp.float32),
        "compress": gaussian(key_list[8], (NODES, RANK), NODES ** -0.5, 0.4375, (), jnp.float32),
        "expand": gaussian(key_list[9], (NODES, RANK), RANK ** -0.5, 1.0, (), jnp.float32),
    }


highest = lax.Precision.HIGHEST
parent_scale = 0.5
summit_scale = 0.25


def offset_list():
    listing = []
    for shift_x in range(-3, 4):
        for shift_y in range(-3, 4):
            for shift_z in range(-3, 4):
                if max(abs(shift_x), abs(shift_y), abs(shift_z)) > 1:
                    listing.append((shift_x, shift_y, shift_z))
    return listing


def chebyshev_terms(values, degree_count):
    firsts = [jnp.ones_like(values), values]
    slopes = [jnp.zeros_like(values), jnp.ones_like(values)]
    for degree in range(2, degree_count):
        firsts.append(2.0 * values * firsts[-1] - firsts[-2])
        slopes.append(2.0 * firsts[-2] + 2.0 * values * slopes[-1] - slopes[-2])
    return jnp.stack(firsts[:degree_count]), jnp.stack(slopes[:degree_count])


def basis_coefficients(node_order):
    angles = (2.0 * np.arange(node_order) + 1.0) * np.pi / (2.0 * node_order)
    degrees = np.arange(node_order)
    weights = np.where(degrees == 0, 1.0, 2.0) / node_order
    basis_table = np.cos(angles[:, None] * degrees[None, :]) * weights[None, :]
    return jnp.asarray(basis_table, jnp.float32), np.cos(angles)


def child_operators(node_order):
    basis_table, node_points = basis_coefficients(node_order)
    inside = jnp.asarray(np.stack([(node_points - 1.0) / 2.0, (node_points + 1.0) / 2.0]), jnp.float32)
    values, slopes = chebyshev_terms(inside, node_order)
    return jnp.einsum('ik,ksa->sia', basis_table, values, precision=highest)


def multipole_block(coords, normals, charges, basis_table, node_order):
    values, slopes = chebyshev_terms(coords, node_order)
    interp = jnp.einsum('ak,kdls->adls', basis_table, values, precision=highest)
    derivative = jnp.einsum('ak,kdls->adls', basis_table, slopes, precision=highest)
    along_x = jnp.einsum('als,bls,cls,rls->lrabc', derivative[:, 0], interp[:, 1], interp[:, 2], charges * normals[0][None], precision=highest)
    along_y = jnp.einsum('als,bls,cls,rls->lrabc', interp[:, 0], derivative[:, 1], interp[:, 2], charges * normals[1][None], precision=highest)
    along_z = jnp.einsum('als,bls,cls,rls->lrabc', interp[:, 0], interp[:, 1], derivative[:, 2], charges * normals[2][None], precision=highest)
    summed = along_x + along_y + along_z
    return summed.reshape(summed.shape[0], summed.shape[1], node_order ** 3), interp


def potential_block(interp, field, node_order):
    grouped = field.reshape(field.shape[0], field.shape[1], node_order, node_order, node_order)
    return jnp.einsum('lrabc,als,bls,cls->rls', grouped, interp[:, 0], interp[:, 1], interp[:, 2], precision=highest)


def merge_children(poles, children, node_order):
    extent_x, extent_z, extent_y, rhs_count, node_count = poles.shape
    grouped = poles.reshape(extent_x // 2, 2, extent_z // 2, 2, extent_y // 2, 2, rhs_count, node_order, node_order, node_order)
    merged = jnp.einsum('xpzqyvrabc,pia,vjb,qlc->xzyrijl', grouped, children, children, children, precision=highest)
    return merged.reshape(extent_x // 2, extent_z // 2, extent_y // 2, rhs_count, node_count)


def spread_children(field, children, node_order):
    extent_x, extent_z, extent_y, rhs_count, node_count = field.shape
    grouped = field.reshape(extent_x, extent_z, extent_y, rhs_count, node_order, node_order, node_order)
    spread = jnp.einsum('xzyrijl,pia,vjb,qlc->xpzqyvrabc', grouped, children, children, children, precision=highest)
    return spread.reshape(2 * extent_x, 2 * extent_z, 2 * extent_y, rhs_count, node_count)


def compress_level(poles, compress):
    coefficient = jnp.einsum('xzyrn,nk->xzyrk', poles, compress, precision=highest)
    return coefficient.reshape(coefficient.shape[0], coefficient.shape[1], -1)


def expand_level(local_part, expand):
    return jnp.einsum('xzyrk,nk->xzyrn', local_part, expand, precision=highest)


def widen_y(extended, extent_y, columns):
    first_size, second_size = extended.shape[0], extended.shape[1]
    grouped = extended.reshape(first_size, second_size, extent_y, columns)
    grouped = jnp.pad(grouped, ((0, 0), (0, 0), (3, 3), (0, 0)))
    return grouped.reshape(first_size, second_size, (extent_y + 6) * columns)


def translate_level(extended, listing, translations, factor, extents):
    span_x, span_z, span_y, rhs_count, rank_size = extents
    offsets = offset_list()
    columns = rhs_count * rank_size
    selectors = jnp.moveaxis(listing.reshape(span_x, span_z, span_y, len(offsets)), 3, 1).astype(jnp.float32)

    def one_plane(inputs):
        position, mask_plane = inputs
        window = lax.dynamic_slice_in_dim(extended, position, 7, 0)
        total = jnp.zeros((span_z, span_y, rhs_count, rank_size), jnp.float32)
        for shift_group in range(-3, 4):
            chosen = [index for index in range(len(offsets)) if offsets[index][0] == shift_group]
            first, last = chosen[0], chosen[-1] + 1
            pieces = [window[3 + offsets[index][0], 3 + offsets[index][2]:3 + offsets[index][2] + span_z, (3 + offsets[index][1]) * columns:(3 + offsets[index][1] + span_y) * columns] for index in chosen]
            stacked = jnp.stack(pieces).reshape(len(chosen), span_z, span_y, rhs_count, rank_size)
            stacked = stacked * mask_plane[first:last, :, :, None, None]
            total = total + jnp.einsum('ozyrk,oik->zyri', stacked, translations[first:last], precision=highest)
        return total

    result = lax.map(one_plane, (jnp.arange(span_x, dtype=jnp.int32), selectors))
    return factor * result


def to_grid(values, extent_x, extent_z):
    columns = values.shape[-1]
    grouped = values.reshape(N_BLOCK, N_SLAB, extent_x, extent_z, columns)
    grouped = jnp.transpose(grouped, (0, 2, 1, 3, 4))
    return grouped.reshape(N_BLOCK * extent_x, N_SLAB * extent_z, columns)


def from_grid(values, extent_x, extent_z):
    columns = values.shape[-1]
    grouped = values.reshape(N_BLOCK, extent_x, N_SLAB, extent_z, columns)
    grouped = jnp.transpose(grouped, (0, 2, 1, 3, 4))
    return grouped.reshape(N_BLOCK * N_SLAB, extent_x, extent_z, columns)


def reference(point_coords, point_normals, strengths, point_counts, leaf_list, parent_list, summit_list, translations, compress, expand):
    node_order = ORDER
    basis_table, node_points = basis_coefficients(node_order)
    children = child_operators(node_order)
    devices = N_BLOCK * N_SLAB
    columns = RHS * RANK
    leaf_count = BX * BZ * SY

    def per_device(values):
        return jnp.moveaxis(values.reshape(values.shape[0], devices, -1), 1, 0)

    def by_plane(values):
        return jnp.moveaxis(values.reshape(values.shape[0], BX, BZ * SY, PCAP), 1, 0)

    filled = (jnp.arange(PCAP, dtype=jnp.int32)[None, None, :] < point_counts[:, :, None]).astype(jnp.float32)
    charges = strengths.reshape(RHS, devices, leaf_count, PCAP) * filled[None]
    charges = jnp.moveaxis(charges, 1, 0).reshape(devices, RHS, leaf_count * PCAP)

    def upward(inputs):
        coords, normals, loads = inputs

        def plane_poles(pieces):
            return multipole_block(pieces[0], pieces[1], pieces[2], basis_table, node_order)[0]

        poles = lax.map(plane_poles, (by_plane(coords), by_plane(normals), by_plane(loads)))
        leaf_poles = poles.reshape(BX, BZ, SY, RHS, -1)
        parent_poles = merge_children(leaf_poles, children, node_order)
        summit_poles = merge_children(parent_poles, children, node_order)
        return compress_level(leaf_poles, compress), compress_level(parent_poles, compress), compress_level(summit_poles, compress)

    leaf_coef, parent_coef, summit_coef = lax.map(upward, (per_device(point_coords), per_device(point_normals), charges))

    def level_locals(coefficient, listing, extent_x, extent_z, extent_y, factor):
        grid = to_grid(coefficient, extent_x, extent_z)
        padded = widen_y(jnp.pad(grid, ((3, 3), (3, 3), (0, 0))), extent_y, columns)
        list_grid = to_grid(listing.reshape(devices, extent_x, extent_z, extent_y * OFFSETS), extent_x, extent_z)
        list_grid = list_grid.reshape(-1, OFFSETS)
        result = translate_level(padded, list_grid, translations, factor, (grid.shape[0], grid.shape[1], extent_y, RHS, RANK))
        return from_grid(result.reshape(grid.shape[0], grid.shape[1], -1), extent_x, extent_z)

    leaf_local = level_locals(leaf_coef, leaf_list, BX, BZ, SY, 1.0)
    parent_local = level_locals(parent_coef, parent_list, BX // 2, BZ // 2, SY // 2, parent_scale)
    summit_local = level_locals(summit_coef, summit_list, BX // 4, BZ // 4, SY // 4, summit_scale)

    def downward(inputs):
        coords, leaf_part, parent_part, summit_part = inputs
        summit_field = expand_level(summit_part.reshape(BX // 4, BZ // 4, SY // 4, RHS, RANK), expand)
        parent_field = expand_level(parent_part.reshape(BX // 2, BZ // 2, SY // 2, RHS, RANK), expand) + spread_children(summit_field, children, node_order)
        leaf_field = expand_level(leaf_part.reshape(BX, BZ, SY, RHS, RANK), expand) + spread_children(parent_field, children, node_order)

        def plane_potential(pieces):
            plane_coords, plane_field = pieces
            values, slopes = chebyshev_terms(plane_coords, node_order)
            interp = jnp.einsum('ak,kdls->adls', basis_table, values, precision=highest)
            return potential_block(interp, plane_field, node_order)

        result = lax.map(plane_potential, (by_plane(coords), leaf_field.reshape(BX, BZ * SY, RHS, -1)))
        return jnp.moveaxis(result, 0, 1).reshape(RHS, -1)

    potential = lax.map(downward, (per_device(point_coords), leaf_local, parent_local, summit_local))
    return jnp.moveaxis(potential, 0, 1).reshape(RHS, -1)
```

```python
import functools

import jax
import jax.numpy as jnp
import ml_dtypes
import numpy as np
from jax import lax
from jax.experimental import pallas as pl
from jax.experimental.pallas import tpu as pltpu
from jax.sharding import PartitionSpec as P

ORDER = 6
NODES = ORDER**3
RANK = 32
RHS = 2
BX, BZ, SY = 8, 8, 4
PCAP = 16
LEAVES = BX * BZ * SY
CHUNK = 256
f32 = jnp.float32
bf16 = jnp.bfloat16
VMEM_LIMIT = 56 * 1024 * 1024


def np_split(values):
    high = values.astype(np.float32).astype(ml_dtypes.bfloat16)
    low = (values - high.astype(np.float64)).astype(np.float32).astype(ml_dtypes.bfloat16)
    return high, low


def basis_table():
    angles = (2.0 * np.arange(ORDER) + 1.0) * np.pi / (2.0 * ORDER)
    degrees = np.arange(ORDER)
    weights = np.where(degrees == 0, 1.0, 2.0) / ORDER
    return np.cos(angles[:, None] * degrees[None, :]) * weights[None, :], np.cos(angles)


def basis_expander():
    table, _ = basis_table()
    full = np.zeros((3, NODES, ORDER, 8))
    for node in range(NODES):
        parts = (node // 36, node // 6 % 6, node % 6)
        for dim in range(3):
            full[dim, node, :, dim] = table[parts[dim]]
    high, low = np_split(full.reshape(3 * NODES, ORDER * 8))
    return np.concatenate([high, low, high], axis=1)


def child_kron():
    table, nodes = basis_table()
    sides = []
    for side in range(2):
        inside = (nodes + 2 * side - 1.0) / 2.0
        terms = np.cos(np.arange(ORDER)[:, None] * np.arccos(inside)[None, :])
        sides.append(table @ terms)
    stack = []
    for hx in range(2):
        for hz in range(2):
            for hy in range(2):
                full = np.einsum("ia,jb,lc->ijlabc", sides[hx], sides[hy], sides[hz])
                stack.append(full.reshape(NODES, NODES))
    return np.stack(stack)


def leaf_column(x, z, y, r):
    child = (x % 2) * 4 + (z % 2) * 2 + y % 2
    return child * 64 + parent_column(x // 2, z // 2, y // 2, r)


def parent_column(x, z, y, r):
    inner = (x % 2) * 4 + (z % 2) * 2 + y % 2
    return inner * 8 + r * 4 + (x // 2) * 2 + z // 2


@functools.lru_cache(None)
def tables():
    out = {}
    code = np.zeros((1, 512), np.int32)
    perm_leaf = np.zeros((512, 512), np.float32)
    perm_parent = np.zeros((64, 256), np.float32)
    perm_top = np.zeros((8, 128), np.float32)
    place = np.zeros((8, 192, 256), np.float32)
    target = np.full((2, 7, 7, 128), -1, np.int32)
    back = np.zeros((4, 128, 512), np.float32)
    back_parent = np.zeros((128, 64), np.float32)
    back_top = np.zeros((128, 8), np.float32)
    select = np.zeros((LEAVES, 512), np.float32)
    select_parent = np.zeros((32, 128), np.float32)
    select_top = np.zeros((4, 128), np.float32)
    for r in range(2):
        for x in range(8):
            for z in range(8):
                for y in range(4):
                    box = x * 32 + z * 4 + y
                    column = leaf_column(x, z, y, r)
                    code[0, column] = box * 2 + r
                    perm_leaf[column, x * 64 + r * 32 + z * 4 + y] = 1
                    half, inner = x // 4, x % 4
                    lane = half * 64 + r * 32 + z * 4 + y
                    back[inner, lane, column] = 1
                    select[box, inner * 128 + lane] = 1
                    for sy in range(7):
                        for sz in range(7):
                            yy, ze = y + sy - 3, z + sz - 1
                            if 0 <= yy < 4 and 0 <= ze < 12:
                                target[0, sy, sz, lane] = half * 128 + r * 48 + ze * 4 + yy
        for x in range(4):
            for z in range(4):
                for y in range(2):
                    column = parent_column(x, z, y, r)
                    perm_parent[column, x * 64 + r * 8 + z * 2 + y] = 1
                    lane = x * 16 + r * 8 + z * 2 + y
                    back_parent[lane, column] = 1
                    select_parent[x * 8 + z * 2 + y, lane] = 1
                    for sy in range(7):
                        for sz in range(7):
                            yy, ze = y + sy - 3, z + sz - 1
                            if 0 <= yy < 2 and 0 <= ze < 8:
                                target[1, sy, sz, lane] = x * 32 + r * 16 + ze * 2 + yy
        for x in range(2):
            for z in range(2):
                column = r * 4 + x * 2 + z
                perm_top[column, x * 64 + r * 2 + z] = 1
                lane = 64 + x * 4 + r * 2 + z
                back_top[lane, column] = 1
                select_top[x * 2 + z, lane] = 1
                for sz in range(7):
                    ze = z + sz - 1
                    if 0 <= ze < 6:
                        target[1, 3, sz, lane] = 128 + x * 16 + r * 6 + ze
        for half in range(2):
            for ze in range(12):
                for y in range(4):
                    slab, z = (ze + 6) // 8, (ze + 6) % 8
                    place[half, slab * 64 + r * 32 + z * 4 + y, half * 128 + r * 48 + ze * 4 + y] = 1
        for x in range(4):
            for ze in range(8):
                for y in range(2):
                    slab, z = (ze + 2) // 4, (ze + 2) % 4
                    place[2 + x, slab * 64 + r * 8 + z * 2 + y, x * 32 + r * 16 + ze * 2 + y] = 1
        for x in range(2):
            for ze in range(6):
                slab, z = ze // 2, ze % 2
                place[6 + x, slab * 64 + r * 2 + z, 128 + x * 16 + r * 6 + ze] = 1
    pad = np.zeros((343, 316), np.float32)
    index = 0
    for full in range(343):
        shifts = (full // 49 - 3, full // 7 % 7 - 3, full % 7 - 3)
        if max(abs(s) for s in shifts) > 1:
            pad[full, index] = 1
            index += 1
    low = lambda a: a.astype(ml_dtypes.bfloat16)
    kron = child_kron()
    out["kron"] = np.stack(np_split(kron))
    out["kron_t"] = np.stack(np_split(np.swapaxes(kron, 1, 2)))
    out["expander"] = basis_expander()
    out["code"] = code
    out["target"] = target
    for name, table in (
        ("perm_leaf", perm_leaf),
        ("perm_parent", perm_parent),
        ("perm_top", perm_top),
        ("place", place),
        ("back", back),
        ("back_parent", back_parent),
        ("back_top", back_top),
        ("select", select),
        ("select_parent", select_parent),
        ("select_top", select_top),
        ("pad", pad),
    ):
        out[name] = low(table)
    return out


def split(values):
    high = values.astype(bf16)
    return high, (values - high.astype(f32)).astype(bf16)


def dot(a, b):
    return jnp.dot(a, b, preferred_element_type=f32)


def dot2(a, exact):
    high, low = split(a)
    return dot(high, exact) + dot(low, exact)


def dot3(a, b):
    a_high, a_low = a
    b_high, b_low = b
    return dot(a_high, b_high) + dot(a_low, b_high) + dot(a_high, b_low)


def degree_rows(coords, normals):
    firsts = [jnp.ones_like(coords), coords]
    slopes = [jnp.zeros_like(coords), jnp.ones_like(coords)]
    for _ in range(2, ORDER):
        firsts.append(2.0 * coords * firsts[-1] - firsts[-2])
        slopes.append(2.0 * firsts[-2] + 2.0 * coords * slopes[-1] - slopes[-2])

    def rows(parts):
        high, low = split(jnp.concatenate(parts, axis=0))
        return jnp.concatenate([high, high, low], axis=0)

    if normals is None:
        return rows(firsts), None
    return rows(firsts), rows([slope * normals for slope in slopes])


def thirds(values):
    return values[:NODES], values[NODES : 2 * NODES], values[2 * NODES :]


def upward_kernel(
    coords, normals, charges, expander, code, kron, compress_t, perm_leaf, perm_parent, perm_top, out, poles
):
    poles[...] = jnp.zeros_like(poles)

    def chunk(step, _):
        lanes = pl.ds(pl.multiple_of(step * CHUNK, CHUNK), CHUNK)
        value_rows, slope_rows = degree_rows(coords[:, lanes], normals[:, lanes])
        sx, sy, sz = thirds(dot(expander[...], value_rows))
        dx, dy, dz = thirds(dot(expander[...], slope_rows))
        basis = dx * (sy * sz) + sx * (dy * sz + sy * dz)
        leaf = lax.broadcasted_iota(jnp.int32, (CHUNK, 512), 0) // PCAP + step * (CHUNK // PCAP)
        total = poles[...]
        for r in range(RHS):
            one_hot = (leaf * 2 + r == code[...]).astype(f32).astype(bf16)
            total = total + dot2(basis * charges[r : r + 1, lanes], one_hot)
        poles[...] = total
        return 0

    lax.fori_loop(0, coords.shape[1] // CHUNK, chunk, 0)
    weights = split(compress_t[...])
    leaf_poles = poles[...]
    leaf_coef = dot2(dot3(weights, split(leaf_poles)), perm_leaf[...])
    parent_poles = jnp.zeros((NODES, 64), f32)
    for h in range(8):
        parent_poles = parent_poles + dot3(
            (kron[0, h], kron[1, h]), split(leaf_poles[:, h * 64 : h * 64 + 64])
        )
    parent_coef = dot2(dot3(weights, split(parent_poles)), perm_parent[...])
    top_poles = jnp.zeros((NODES, 8), f32)
    for h in range(8):
        top_poles = top_poles + dot3(
            (kron[0, h], kron[1, h]), split(parent_poles[:, h * 8 : h * 8 + 8])
        )
    top_coef = dot2(dot3(weights, split(top_poles)), perm_top[...])
    for x in range(8):
        out[x] = leaf_coef[:, x * 64 : x * 64 + 64]
    for x in range(4):
        out[8 + x] = parent_coef[:, x * 64 : x * 64 + 64]
    for x in range(2):
        out[12 + x] = top_coef[:, x * 64 : x * 64 + 64]


def downward_kernel(
    full,
    place,
    target,
    operators,
    mask,
    back,
    back_parent,
    back_top,
    expand,
    kron_t,
    coords,
    expander,
    code_column,
    out,
    src_high,
    src_low,
    coarse_high,
    coarse_low,
    ops,
    parent_field,
    leaf_field,
    field_high,
    field_low,
):
    def load_ops(index, _):
        high, low = split(operators[index])
        ops[index, :32] = high
        ops[index, 32:] = low
        return 0

    lax.fori_loop(0, 49, load_ops, 0)

    def gathered(pieces, rows):
        high = jnp.zeros((rows, 256), f32)
        low = jnp.zeros((rows, 256), f32)
        for start, slot in pieces:
            part_high, part_low = split(full[start * 32 : start * 32 + rows])
            high = high + dot(part_high, place[slot])
            low = low + dot(part_low, place[slot])
        return high.astype(bf16), low.astype(bf16)

    leaf_src = gathered([(0, 0), (4, 1)], 256)
    coarse_src = gathered(
        [(12, 2), (13, 3), (14, 4), (15, 5), (22, 6), (23, 7)], 224
    )
    row_ids = lax.broadcasted_iota(jnp.int32, (256, 128), 0)
    for level, source, refs in (
        (0, leaf_src, (src_high, src_low)),
        (1, coarse_src, (coarse_high, coarse_low)),
    ):
        count = source[0].shape[0] // 32
        for sy in range(7):
            for sz in range(7):
                one_hot = (row_ids == target[level, sy, sz : sz + 1]).astype(f32).astype(bf16)
                for values, ref in zip(source, refs):
                    moved = dot(values, one_hot).astype(bf16)
                    ref[:, sy, sz * 32 : sz * 32 + 32] = moved.reshape(count, 32, 128)

    def shifted(high_ref, low_ref, xb, sx, first, carry):
        both, cross = carry
        for sy in range(7):
            rows = mask[sx, sy * 7 : sy * 7 + 7, first : first + 128]
            chosen = jnp.concatenate(
                [jnp.broadcast_to(rows[i : i + 1], (32, 128)) for i in range(7)], axis=0
            ).astype(bf16)
            weights = ops[sx * 7 + sy]
            both = both + dot(weights, high_ref[xb, sy] * chosen)
            cross = cross + dot(weights[:32], low_ref[xb, sy] * chosen)
        return both, cross

    def finish(carry):
        both, cross = carry
        return both[:32] + both[32:] + cross

    zeros = (jnp.zeros((64, 128), f32), jnp.zeros((32, 128), f32))
    leaf_local = jnp.zeros((32, 512), f32)
    for xi in range(4):
        begin = 1 - xi % 2

        def step(t, carry, xi=xi, begin=begin):
            sx = t + begin
            return shifted(src_high, src_low, xi + sx - 1, sx, xi * 128, carry)

        local = finish(lax.fori_loop(0, 6, step, zeros))
        leaf_local = leaf_local + dot2(local, back[xi])

    def coarse_step(sx, carry):
        return shifted(coarse_high, coarse_low, sx, sx, 512, carry)

    coarse = finish(lax.fori_loop(0, 7, coarse_step, zeros))
    weights = split(expand[...])
    top_field = dot3(weights, split(0.25 * dot2(coarse, back_top[...])))
    parent_own = dot3(weights, split(0.5 * dot2(coarse, back_parent[...])))
    parts = split(top_field)
    for h in range(8):
        cols = slice(h * 8, h * 8 + 8)
        parent_field[:, cols] = parent_own[:, cols] + dot3((kron_t[0, h], kron_t[1, h]), parts)
    leaf_own = dot3(weights, split(leaf_local))
    parts = split(parent_field[...])
    for h in range(8):
        cols = slice(h * 64, h * 64 + 64)
        leaf_field[:, cols] = leaf_own[:, cols] + dot3((kron_t[0, h], kron_t[1, h]), parts)
    field_high[...], field_low[...] = split(leaf_field[...])

    def chunk(index, _):
        lanes = pl.ds(pl.multiple_of(index * CHUNK, CHUNK), CHUNK)
        value_rows, _ = degree_rows(coords[:, lanes], None)
        sx, sy, sz = thirds(dot(expander[...], value_rows))
        basis = sx * (sy * sz)
        leaf = lax.broadcasted_iota(jnp.int32, (512, CHUNK), 1) // PCAP + index * (CHUNK // PCAP)
        for r in range(RHS):
            one_hot = (leaf * 2 + r == code_column[...]).astype(f32).astype(bf16)
            at_points = dot(field_high[...], one_hot) + dot(field_low[...], one_hot)
            out[r : r + 1, lanes] = jnp.sum(basis * at_points, axis=0, keepdims=True)
        return 0

    lax.fori_loop(0, coords.shape[1] // CHUNK, chunk, 0)


def neighbours(tail, head, axis):
    count = lax.axis_size(axis)
    before = lax.ppermute(tail, axis, [(i, i + 1) for i in range(count - 1)])
    after = lax.ppermute(head, axis, [(i + 1, i) for i in range(count - 1)])
    return before, after


def body(
    point_coords,
    point_normals,
    strengths,
    point_counts,
    leaf_list,
    parent_list,
    summit_list,
    translations,
    compress,
    expand,
):
    t = {name: jnp.asarray(value) for name, value in tables().items()}
    points = point_coords.shape[1]
    vmem = pl.BlockSpec(memory_space=pltpu.VMEM)
    params = pltpu.CompilerParams(vmem_limit_bytes=VMEM_LIMIT)
    coords = jnp.pad(point_coords, ((0, 5), (0, 0)))
    normals = jnp.pad(point_normals, ((0, 5), (0, 0)))
    slots = jnp.arange(PCAP, dtype=jnp.int32)[None, :] < point_counts.reshape(-1, 1)
    charges = jnp.where(slots.reshape(1, points), strengths, 0.0)

    coef = pl.pallas_call(
        upward_kernel,
        out_shape=jax.ShapeDtypeStruct((14, RANK, 64), f32),
        in_specs=[vmem] * 10,
        out_specs=vmem,
        scratch_shapes=[pltpu.VMEM((NODES, 512), f32)],
        compiler_params=params,
    )(
        coords,
        normals,
        charges,
        t["expander"],
        t["code"],
        t["kron"],
        compress.T,
        t["perm_leaf"],
        t["perm_parent"],
        t["perm_top"],
    )

    tail = jnp.concatenate([coef[6:8], coef[10:14]])
    head = jnp.concatenate([coef[0:2], coef[8:10], coef[12:14]])
    before, after = neighbours(tail, head, "block")
    blank = jnp.zeros_like(coef[:1])
    ext = jnp.concatenate(
        [before[0:2], coef[0:8], after[0:2], blank, before[2:4], coef[8:12], after[2:4], blank]
        + [blank, before[4:6], coef[12:14], after[4:6], blank]
    )
    left, right = neighbours(ext, ext, "slab")
    full = jnp.concatenate([left, ext, right], axis=2).reshape(30 * RANK, 192)

    def chosen(listing, select):
        return jnp.einsum("bo,bl->ol", listing.astype(bf16), select, preferred_element_type=f32)

    masks = jnp.concatenate(
        [
            chosen(leaf_list, t["select"]),
            chosen(parent_list, t["select_parent"]) + chosen(summit_list, t["select_top"]),
        ],
        axis=1,
    ).astype(bf16)
    masks = jnp.dot(t["pad"], masks, preferred_element_type=f32).reshape(7, 49, 640)
    pieces, index = [], 0
    near = [n for n in range(343) if not tables()["pad"][n].astype(np.float32).any()]
    position = 0
    while position < 343:
        stop = position
        if position in near:
            while stop in near:
                stop += 1
            pieces.append(jnp.zeros((stop - position, RANK, RANK), f32))
        else:
            while stop < 343 and stop not in near:
                stop += 1
            pieces.append(translations[index : index + stop - position])
            index += stop - position
        position = stop
    operators = jnp.concatenate(pieces).reshape(49, 7, RANK, RANK)
    operators = jnp.transpose(operators, (0, 2, 1, 3)).reshape(49, RANK, 7 * RANK)

    return pl.pallas_call(
        downward_kernel,
        out_shape=jax.ShapeDtypeStruct((RHS, points), f32),
        in_specs=[vmem] * 13,
        out_specs=vmem,
        scratch_shapes=[
            pltpu.VMEM((8, 7, 224, 128), bf16),
            pltpu.VMEM((8, 7, 224, 128), bf16),
            pltpu.VMEM((7, 7, 224, 128), bf16),
            pltpu.VMEM((7, 7, 224, 128), bf16),
            pltpu.VMEM((49, 64, 224), bf16),
            pltpu.VMEM((NODES, 64), f32),
            pltpu.VMEM((NODES, 512), f32),
            pltpu.VMEM((NODES, 512), bf16),
            pltpu.VMEM((NODES, 512), bf16),
        ],
        compiler_params=params,
    )(
        full,
        t["place"],
        t["target"],
        operators,
        masks,
        t["back"],
        t["back_parent"],
        t["back_top"],
        expand,
        t["kron_t"],
        coords,
        t["expander"],
        t["code"].reshape(512, 1),
    )


def solution(mesh):
    return jax.shard_map(
        body,
        mesh=mesh,
        in_specs=(
            P(None, ("groups", "block", "slab")),
            P(None, ("groups", "block", "slab")),
            P(None, ("groups", "block", "slab")),
            P(("groups", "block", "slab"), None),
            P(("groups", "block", "slab"), None),
            P(("groups", "block", "slab"), None),
            P(("groups", "block", "slab"), None),
            P(),
            P(),
            P(),
        ),
        out_specs=P(None, ("groups", "block", "slab")),
        check_vma=False,
    )
```

```python
import functools

import jax
import jax.numpy as jnp
import ml_dtypes
import numpy as np
from jax import lax
from jax.experimental import pallas as pl
from jax.experimental.pallas import tpu as pltpu
from jax.sharding import PartitionSpec as P

ORDER = 6
NODES = ORDER**3
RANK = 32
RHS = 2
BX, BZ, SY = 8, 8, 4
PCAP = 16
LEAVES = BX * BZ * SY
CHUNK = 256
f32 = jnp.float32
bf16 = jnp.bfloat16
VMEM_LIMIT = 56 * 1024 * 1024


def np_split(values):
    high = values.astype(np.float32).astype(ml_dtypes.bfloat16)
    low = (values - high.astype(np.float64)).astype(np.float32).astype(ml_dtypes.bfloat16)
    return high, low


def basis_table():
    angles = (2.0 * np.arange(ORDER) + 1.0) * np.pi / (2.0 * ORDER)
    degrees = np.arange(ORDER)
    weights = np.where(degrees == 0, 1.0, 2.0) / ORDER
    return np.cos(angles[:, None] * degrees[None, :]) * weights[None, :], np.cos(angles)


def basis_expander():
    table, _ = basis_table()
    full = np.zeros((3, NODES, ORDER, 8))
    for node in range(NODES):
        parts = (node // 36, node // 6 % 6, node % 6)
        for dim in range(3):
            full[dim, node, :, dim] = table[parts[dim]]
    high, low = np_split(full.reshape(3 * NODES, ORDER * 8))
    return np.concatenate([high, low, high], axis=1)


def child_kron():
    table, nodes = basis_table()
    sides = []
    for side in range(2):
        inside = (nodes + 2 * side - 1.0) / 2.0
        terms = np.cos(np.arange(ORDER)[:, None] * np.arccos(inside)[None, :])
        sides.append(table @ terms)
    stack = []
    for hx in range(2):
        for hz in range(2):
            for hy in range(2):
                full = np.einsum("ia,jb,lc->ijlabc", sides[hx], sides[hy], sides[hz])
                stack.append(full.reshape(NODES, NODES))
    return np.stack(stack)


def leaf_column(x, z, y, r):
    child = (x % 2) * 4 + (z % 2) * 2 + y % 2
    return child * 64 + parent_column(x // 2, z // 2, y // 2, r)


def parent_column(x, z, y, r):
    inner = (x % 2) * 4 + (z % 2) * 2 + y % 2
    return inner * 8 + r * 4 + (x // 2) * 2 + z // 2


@functools.lru_cache(None)
def tables():
    out = {}
    code = np.zeros((1, 512), np.int32)
    perm_leaf = np.zeros((512, 512), np.float32)
    perm_parent = np.zeros((64, 256), np.float32)
    perm_top = np.zeros((8, 128), np.float32)
    place = np.zeros((8, 192, 256), np.float32)
    target = np.full((2, 7, 7, 128), -1, np.int32)
    back = np.zeros((4, 128, 512), np.float32)
    back_parent = np.zeros((128, 64), np.float32)
    back_top = np.zeros((128, 8), np.float32)
    select = np.zeros((LEAVES, 512), np.float32)
    select_parent = np.zeros((32, 128), np.float32)
    select_top = np.zeros((4, 128), np.float32)
    for r in range(2):
        for x in range(8):
            for z in range(8):
                for y in range(4):
                    box = x * 32 + z * 4 + y
                    column = leaf_column(x, z, y, r)
                    code[0, column] = box * 2 + r
                    perm_leaf[column, x * 64 + r * 32 + z * 4 + y] = 1
                    half, inner = x // 4, x % 4
                    lane = half * 64 + r * 32 + z * 4 + y
                    back[inner, lane, column] = 1
                    select[box, inner * 128 + lane] = 1
                    for sy in range(7):
                        for sz in range(7):
                            yy, ze = y + sy - 3, z + sz - 1
                            if 0 <= yy < 4 and 0 <= ze < 12:
                                target[0, sy, sz, lane] = half * 128 + r * 48 + ze * 4 + yy
        for x in range(4):
            for z in range(4):
                for y in range(2):
                    column = parent_column(x, z, y, r)
                    perm_parent[column, x * 64 + r * 8 + z * 2 + y] = 1
                    lane = x * 16 + r * 8 + z * 2 + y
                    back_parent[lane, column] = 1
                    select_parent[x * 8 + z * 2 + y, lane] = 1
                    for sy in range(7):
                        for sz in range(7):
                            yy, ze = y + sy - 3, z + sz - 1
                            if 0 <= yy < 2 and 0 <= ze < 8:
                                target[1, sy, sz, lane] = x * 32 + r * 16 + ze * 2 + yy
        for x in range(2):
            for z in range(2):
                column = r * 4 + x * 2 + z
                perm_top[column, x * 64 + r * 2 + z] = 1
                lane = 64 + x * 4 + r * 2 + z
                back_top[lane, column] = 1
                select_top[x * 2 + z, lane] = 1
                for sz in range(7):
                    ze = z + sz - 1
                    if 0 <= ze < 6:
                        target[1, 3, sz, lane] = 128 + x * 16 + r * 6 + ze
        for half in range(2):
            for ze in range(12):
                for y in range(4):
                    slab, z = (ze + 6) // 8, (ze + 6) % 8
                    place[half, slab * 64 + r * 32 + z * 4 + y, half * 128 + r * 48 + ze * 4 + y] = 1
        for x in range(4):
            for ze in range(8):
                for y in range(2):
                    slab, z = (ze + 2) // 4, (ze + 2) % 4
                    place[2 + x, slab * 64 + r * 8 + z * 2 + y, x * 32 + r * 16 + ze * 2 + y] = 1
        for x in range(2):
            for ze in range(6):
                slab, z = ze // 2, ze % 2
                place[6 + x, slab * 64 + r * 2 + z, 128 + x * 16 + r * 6 + ze] = 1
    pad = np.zeros((343, 316), np.float32)
    index = 0
    for full in range(343):
        shifts = (full // 49 - 3, full // 7 % 7 - 3, full % 7 - 3)
        if max(abs(s) for s in shifts) > 1:
            pad[full, index] = 1
            index += 1
    low = lambda a: a.astype(ml_dtypes.bfloat16)
    kron = child_kron()
    out["kron"] = np.stack(np_split(kron))
    out["kron_t"] = np.stack(np_split(np.swapaxes(kron, 1, 2)))
    out["expander"] = basis_expander()
    out["code"] = code
    out["target"] = target
    for name, table in (
        ("perm_leaf", perm_leaf),
        ("perm_parent", perm_parent),
        ("perm_top", perm_top),
        ("place", place),
        ("back", back),
        ("back_parent", back_parent),
        ("back_top", back_top),
        ("select", select),
        ("select_parent", select_parent),
        ("select_top", select_top),
        ("pad", pad),
    ):
        out[name] = low(table)
    return out


def split(values):
    high = values.astype(bf16)
    return high, (values - high.astype(f32)).astype(bf16)


def dot(a, b):
    return jnp.dot(a, b, preferred_element_type=f32)


def dot2(a, exact):
    high, low = split(a)
    return dot(high, exact) + dot(low, exact)


def dot3(a, b):
    a_high, a_low = a
    b_high, b_low = b
    return dot(a_high, b_high) + dot(a_low, b_high) + dot(a_high, b_low)


def degree_rows(coords, normals):
    firsts = [jnp.ones_like(coords), coords]
    slopes = [jnp.zeros_like(coords), jnp.ones_like(coords)]
    for _ in range(2, ORDER):
        firsts.append(2.0 * coords * firsts[-1] - firsts[-2])
        slopes.append(2.0 * firsts[-2] + 2.0 * coords * slopes[-1] - slopes[-2])

    def rows(parts):
        high, low = split(jnp.concatenate(parts, axis=0))
        return jnp.concatenate([high, high, low], axis=0)

    if normals is None:
        return rows(firsts), None
    return rows(firsts), rows([slope * normals for slope in slopes])


def padded(values):
    return jnp.concatenate([values, jnp.zeros((5, values.shape[1]), f32)], axis=0)


def thirds(values):
    return values[:NODES], values[NODES : 2 * NODES], values[2 * NODES :]


def upward_kernel(
    coords, normals, charges, expander, code, kron, compress_t, perm_leaf, perm_parent, perm_top, out, poles
):
    poles[...] = jnp.zeros_like(poles)

    def chunk(step, _):
        lanes = pl.ds(pl.multiple_of(step * CHUNK, CHUNK), CHUNK)
        value_rows, slope_rows = degree_rows(padded(coords[:, lanes]), padded(normals[:, lanes]))
        sx, sy, sz = thirds(dot(expander[...], value_rows))
        dx, dy, dz = thirds(dot(expander[...], slope_rows))
        basis = dx * (sy * sz) + sx * (dy * sz + sy * dz)
        leaf = lax.broadcasted_iota(jnp.int32, (CHUNK, 512), 0) // PCAP + step * (CHUNK // PCAP)
        total = poles[...]
        for r in range(RHS):
            one_hot = (leaf * 2 + r == code[...]).astype(f32).astype(bf16)
            total = total + dot2(basis * charges[r : r + 1, lanes], one_hot)
        poles[...] = total
        return 0

    lax.fori_loop(0, coords.shape[1] // CHUNK, chunk, 0)
    weights = split(compress_t[...])
    leaf_poles = poles[...]
    leaf_coef = dot2(dot3(weights, split(leaf_poles)), perm_leaf[...])
    parent_poles = jnp.zeros((NODES, 64), f32)
    for h in range(8):
        parent_poles = parent_poles + dot3(
            (kron[0, h], kron[1, h]), split(leaf_poles[:, h * 64 : h * 64 + 64])
        )
    parent_coef = dot2(dot3(weights, split(parent_poles)), perm_parent[...])
    top_poles = jnp.zeros((NODES, 8), f32)
    for h in range(8):
        top_poles = top_poles + dot3(
            (kron[0, h], kron[1, h]), split(parent_poles[:, h * 8 : h * 8 + 8])
        )
    top_coef = dot2(dot3(weights, split(top_poles)), perm_top[...])
    own = [leaf_coef[:, x * 64 : x * 64 + 64] for x in range(8)]
    own += [parent_coef[:, x * 64 : x * 64 + 64] for x in range(4)]
    own += [top_coef[:, x * 64 : x * 64 + 64] for x in range(2)]
    own = [jnp.concatenate([part[:16], part[16:]], axis=1) for part in own]
    order = [0, 1, 8, 9, 12, 13] + list(range(14)) + [6, 7, 10, 11, 12, 13]
    for row, index in enumerate(order):
        out[row] = own[index]


def exchange_kernel(coef, out, land, send, recv):
    block, slab = lax.axis_index("block"), lax.axis_index("slab")
    blocks, slabs = lax.axis_size("block"), lax.axis_size("slab")
    sides = (
        (block > 0, {"block": block - 1}),
        (block < blocks - 1, {"block": block + 1}),
        (slab > 0, {"slab": slab - 1}),
        (slab < slabs - 1, {"slab": slab + 1}),
    )
    mesh_ids = pl.DeviceIdType.MESH
    barrier = pltpu.get_barrier_semaphore()
    for there, device in sides:

        @pl.when(there)
        def _(device=device):
            pl.semaphore_signal(barrier, inc=1, device_id=device, device_id_type=mesh_ids)

    peers = sum(there.astype(jnp.int32) for there, _ in sides)
    pl.semaphore_wait(barrier, peers)

    def copy(src, dst, index, device):
        return pltpu.make_async_remote_copy(
            src_ref=src,
            dst_ref=dst,
            send_sem=send.at[index],
            recv_sem=recv.at[index],
            device_id=device,
            device_id_type=mesh_ids,
        )

    to_left = copy(coef.at[0:6], land.at[1, 20:26], 0, sides[0][1])
    to_right = copy(coef.at[20:26], land.at[1, 0:6], 1, sides[1][1])
    own_down = copy(coef.at[6:20], land.at[2, 6:20], 2, sides[2][1])
    own_up = copy(coef.at[6:20], land.at[0, 6:20], 3, sides[3][1])
    low_down = copy(land.at[1, 0:6], land.at[2, 0:6], 4, sides[2][1])
    low_up = copy(land.at[1, 0:6], land.at[0, 0:6], 5, sides[3][1])
    high_down = copy(land.at[1, 20:26], land.at[2, 20:26], 6, sides[2][1])
    high_up = copy(land.at[1, 20:26], land.at[0, 20:26], 7, sides[3][1])

    @pl.when(sides[0][0])
    def _():
        to_left.start()

    @pl.when(sides[1][0])
    def _():
        to_right.start()

    @pl.when(sides[2][0])
    def _():
        own_down.start()

    @pl.when(sides[3][0])
    def _():
        own_up.start()

    land[1, 6:20] = coef[6:20]

    @pl.when(block == 0)
    def _():
        land[1, 0:6] = jnp.zeros((6, 16, 128), f32)

    @pl.when(block == blocks - 1)
    def _():
        land[1, 20:26] = jnp.zeros((6, 16, 128), f32)

    @pl.when(slab == 0)
    def _():
        land[0] = jnp.zeros((26, 16, 128), f32)

    @pl.when(slab == slabs - 1)
    def _():
        land[2] = jnp.zeros((26, 16, 128), f32)

    @pl.when(sides[0][0])
    def _():
        to_right.wait_recv()

    @pl.when(sides[1][0])
    def _():
        to_left.wait_recv()

    @pl.when(sides[2][0])
    def _():
        low_down.start()
        high_down.start()

    @pl.when(sides[3][0])
    def _():
        low_up.start()
        high_up.start()

    @pl.when(sides[2][0])
    def _():
        own_up.wait_recv()
        low_up.wait_recv()
        high_up.wait_recv()

    @pl.when(sides[3][0])
    def _():
        own_down.wait_recv()
        low_down.wait_recv()
        high_down.wait_recv()

    out[...] = land[...]

    @pl.when(sides[0][0])
    def _():
        to_left.wait_send()

    @pl.when(sides[1][0])
    def _():
        to_right.wait_send()

    @pl.when(sides[2][0])
    def _():
        own_down.wait_send()
        low_down.wait_send()
        high_down.wait_send()

    @pl.when(sides[3][0])
    def _():
        own_up.wait_send()
        low_up.wait_send()
        high_up.wait_send()


def source_rows():
    leaf = [e if e < 2 else e + 4 if e < 10 else e + 10 for e in range(12)]
    parent = [2 + e if e < 2 else 12 + e if e < 6 else 16 + e for e in range(8)]
    top = [4 + e if e < 2 else 16 + e if e < 4 else 20 + e for e in range(6)]
    return leaf + [None] + parent + [None, None] + top + [None]


def downward_kernel(
    exchanged,
    place,
    target,
    translations,
    mask,
    back,
    back_parent,
    back_top,
    expand,
    kron_t,
    coords,
    expander,
    code_column,
    out,
    full_high,
    full_low,
    src_high,
    src_low,
    coarse_high,
    coarse_low,
    ops,
    parent_field,
    leaf_field,
    field_high,
    field_low,
):
    listed = 0
    for pair in range(49):
        pieces = []
        for sz in range(7):
            shifts = (pair // 7 - 3, pair % 7 - 3, sz - 3)
            if max(abs(s) for s in shifts) > 1:
                pieces.append(translations[listed])
                listed += 1
            else:
                pieces.append(jnp.zeros((32, 32), f32))
        high, low = split(jnp.concatenate(pieces, axis=1))
        ops[pair, :32] = high
        ops[pair, 32:] = low

    for row, source in enumerate(source_rows()):
        for half in range(2):
            rows = slice(row * 32 + half * 16, row * 32 + half * 16 + 16)
            if source is None:
                full_high[rows] = jnp.zeros((16, 192), bf16)
                full_low[rows] = jnp.zeros((16, 192), bf16)
            else:
                lanes = slice(half * 64, half * 64 + 64)
                parts = [exchanged[slab, source, :, lanes] for slab in range(3)]
                full_high[rows], full_low[rows] = split(jnp.concatenate(parts, axis=1))

    def gathered(pieces, rows):
        high = jnp.zeros((rows, 256), f32)
        low = jnp.zeros((rows, 256), f32)
        for start, slot in pieces:
            part = slice(start * 32, start * 32 + rows)
            high = high + dot(full_high[part], place[slot])
            low = low + dot(full_low[part], place[slot])
        return high.astype(bf16), low.astype(bf16)

    leaf_src = gathered([(0, 0), (4, 1)], 256)
    coarse_src = gathered(
        [(12, 2), (13, 3), (14, 4), (15, 5), (22, 6), (23, 7)], 224
    )
    row_ids = lax.broadcasted_iota(jnp.int32, (256, 128), 0)
    for level, source, refs in (
        (0, leaf_src, (src_high, src_low)),
        (1, coarse_src, (coarse_high, coarse_low)),
    ):
        count = source[0].shape[0] // 32
        for sy in range(7):
            for sz in range(7):
                one_hot = (row_ids == target[level, sy, sz : sz + 1]).astype(f32).astype(bf16)
                for values, ref in zip(source, refs):
                    moved = dot(values, one_hot).astype(bf16)
                    ref[:, sy, sz * 32 : sz * 32 + 32] = moved.reshape(count, 32, 128)

    def shifted(high_ref, low_ref, xb, sx, first, carry):
        both, cross = carry
        for sy in range(7):
            rows = mask[sx, sy * 7 : sy * 7 + 7, first : first + 128]
            chosen = jnp.concatenate(
                [jnp.broadcast_to(rows[i : i + 1], (32, 128)) for i in range(7)], axis=0
            ).astype(bf16)
            weights = ops[sx * 7 + sy]
            both = both + dot(weights, high_ref[xb, sy] * chosen)
            cross = cross + dot(weights[:32], low_ref[xb, sy] * chosen)
        return both, cross

    def finish(carry):
        both, cross = carry
        return both[:32] + both[32:] + cross

    zeros = (jnp.zeros((64, 128), f32), jnp.zeros((32, 128), f32))
    leaf_local = jnp.zeros((32, 512), f32)
    for xi in range(4):
        begin = 1 - xi % 2

        def step(t, carry, xi=xi, begin=begin):
            sx = t + begin
            return shifted(src_high, src_low, xi + sx - 1, sx, xi * 128, carry)

        local = finish(lax.fori_loop(0, 6, step, zeros))
        leaf_local = leaf_local + dot2(local, back[xi])

    def coarse_step(sx, carry):
        return shifted(coarse_high, coarse_low, sx, sx, 512, carry)

    coarse = finish(lax.fori_loop(0, 7, coarse_step, zeros))
    weights = split(expand[...])
    top_field = dot3(weights, split(0.25 * dot2(coarse, back_top[...])))
    parent_own = dot3(weights, split(0.5 * dot2(coarse, back_parent[...])))
    parts = split(top_field)
    for h in range(8):
        cols = slice(h * 8, h * 8 + 8)
        parent_field[:, cols] = parent_own[:, cols] + dot3((kron_t[0, h], kron_t[1, h]), parts)
    leaf_own = dot3(weights, split(leaf_local))
    parts = split(parent_field[...])
    for h in range(8):
        cols = slice(h * 64, h * 64 + 64)
        leaf_field[:, cols] = leaf_own[:, cols] + dot3((kron_t[0, h], kron_t[1, h]), parts)
    field_high[...], field_low[...] = split(leaf_field[...])

    def chunk(index, _):
        lanes = pl.ds(pl.multiple_of(index * CHUNK, CHUNK), CHUNK)
        value_rows, _ = degree_rows(padded(coords[:, lanes]), None)
        sx, sy, sz = thirds(dot(expander[...], value_rows))
        basis = sx * (sy * sz)
        leaf = lax.broadcasted_iota(jnp.int32, (512, CHUNK), 1) // PCAP + index * (CHUNK // PCAP)
        for r in range(RHS):
            one_hot = (leaf * 2 + r == code_column[...]).astype(f32).astype(bf16)
            at_points = dot(field_high[...], one_hot) + dot(field_low[...], one_hot)
            out[r : r + 1, lanes] = jnp.sum(basis * at_points, axis=0, keepdims=True)
        return 0

    lax.fori_loop(0, coords.shape[1] // CHUNK, chunk, 0)


def body(
    point_coords,
    point_normals,
    strengths,
    point_counts,
    leaf_list,
    parent_list,
    summit_list,
    translations,
    compress,
    expand,
):
    t = {name: jnp.asarray(value) for name, value in tables().items()}
    points = point_coords.shape[1]
    vmem = pl.BlockSpec(memory_space=pltpu.VMEM)
    params = pltpu.CompilerParams(vmem_limit_bytes=VMEM_LIMIT)
    slots = jnp.arange(PCAP, dtype=jnp.int32)[None, :] < point_counts.reshape(-1, 1)
    charges = jnp.where(slots.reshape(1, points), strengths, 0.0)

    coef = pl.pallas_call(
        upward_kernel,
        out_shape=jax.ShapeDtypeStruct((26, 16, 128), f32),
        in_specs=[vmem] * 10,
        out_specs=vmem,
        scratch_shapes=[pltpu.VMEM((NODES, 512), f32)],
        compiler_params=params,
    )(
        point_coords,
        point_normals,
        charges,
        t["expander"],
        t["code"],
        t["kron"],
        compress.T,
        t["perm_leaf"],
        t["perm_parent"],
        t["perm_top"],
    )

    exchanged = pl.pallas_call(
        exchange_kernel,
        out_shape=jax.ShapeDtypeStruct((3, 26, 16, 128), f32),
        in_specs=[vmem],
        out_specs=vmem,
        scratch_shapes=[
            pltpu.VMEM((3, 26, 16, 128), f32),
            pltpu.SemaphoreType.DMA((8,)),
            pltpu.SemaphoreType.DMA((8,)),
        ],
        compiler_params=pltpu.CompilerParams(collective_id=0, has_side_effects=True),
    )(coef)

    def chosen(listing, select):
        return jnp.einsum("bo,bl->ol", listing.astype(bf16), select, preferred_element_type=f32)

    masks = jnp.concatenate(
        [
            chosen(leaf_list, t["select"]),
            chosen(parent_list, t["select_parent"]) + chosen(summit_list, t["select_top"]),
        ],
        axis=1,
    ).astype(bf16)
    masks = jnp.dot(t["pad"], masks, preferred_element_type=f32).reshape(7, 49, 640)
    return pl.pallas_call(
        downward_kernel,
        out_shape=jax.ShapeDtypeStruct((RHS, points), f32),
        in_specs=[vmem] * 13,
        out_specs=vmem,
        scratch_shapes=[
            pltpu.VMEM((30 * RANK, 192), bf16),
            pltpu.VMEM((30 * RANK, 192), bf16),
            pltpu.VMEM((8, 7, 224, 128), bf16),
            pltpu.VMEM((8, 7, 224, 128), bf16),
            pltpu.VMEM((7, 7, 224, 128), bf16),
            pltpu.VMEM((7, 7, 224, 128), bf16),
            pltpu.VMEM((49, 64, 224), bf16),
            pltpu.VMEM((NODES, 64), f32),
            pltpu.VMEM((NODES, 512), f32),
            pltpu.VMEM((NODES, 512), bf16),
            pltpu.VMEM((NODES, 512), bf16),
        ],
        compiler_params=params,
    )(
        exchanged,
        t["place"],
        t["target"],
        translations,
        masks,
        t["back"],
        t["back_parent"],
        t["back_top"],
        expand,
        t["kron_t"],
        point_coords,
        t["expander"],
        t["code"].reshape(512, 1),
    )


def solution(mesh):
    return jax.shard_map(
        body,
        mesh=mesh,
        in_specs=(
            P(None, ("groups", "block", "slab")),
            P(None, ("groups", "block", "slab")),
            P(None, ("groups", "block", "slab")),
            P(("groups", "block", "slab"), None),
            P(("groups", "block", "slab"), None),
            P(("groups", "block", "slab"), None),
            P(("groups", "block", "slab"), None),
            P(),
            P(),
            P(),
        ),
        out_specs=P(None, ("groups", "block", "slab")),
        check_vma=False,
    )
```
